32 devices in a mesh: cuts: 2 (over y), inter: 16 (over z, x, core).
Axes of the slice: x: 2, y: 2, z: 4, core: 2. Of those that a mesh axis runs over, the one named last changes fastest.
Arguments:
- stem_tensor: bfloat16 [2, 1024, 512, 1, 256], P(None, ('cuts', 'inter')), parts along dimension 1, may hold values from -6 to 6
- branch_one: bfloat16 [2, 512, 512], replicated, may hold values from -0.1875 to 0.1875
- branch_two: bfloat16 [2, 256, 256], replicated, may hold values from -0.25 to 0.25
- mode_order: int32 [256], replicated, may hold values from 0 to 255, each once
- branch_three: bfloat16 [2, 512, 512], replicated, may hold values from -0.1875 to 0.1875
- closing: bfloat16 [2, 512, 512], replicated, may hold values from -4 to 4
Outputs:
- amplitudes: float32 [1024, 512, 2, 1, 256], P(('cuts', 'inter')), parts along dimension 0
The draws below stay inside these ranges and needn't reach their ends.
There are 2 independent parts, one for each index of `cuts`. The reference program is written for one: setup_inputs(seed, part) draws one part's arguments, and reference() takes and returns one part's arrays. A program takes and returns all parts, laid end to end along the dimension named above; an argument that names none is the same for every part. Nothing has to cross between parts.
All inputs are finite; a program needn't handle non-finite values.
Results may differ from the reference program's by a relative error of at most 0.0041.
Values may be sent and summed in bfloat16 or wider, within the bound.
A program may use at most 192 MiB of HBM per device.

```python
import jax
import jax.numpy as jnp
from jax import lax

SWAP_A = 512
SWAP_B = 512
LOCAL_R = 256
AMPS = 1


def level_of(stream_key, extent, split, low, high):
    level, own = 1.0, jax.random.fold_in(stream_key, 6)
    for dim, parts in split:
        steps = jnp.exp(jax.random.uniform(jax.random.fold_in(own, dim), (parts,), jnp.float32, low / len(split), high / len(split)))
        level = level * jnp.repeat(steps, extent[dim] // parts).reshape([-1 if axis == dim else 1 for axis in range(len(extent))])
    return level


def normal_values(own_key, dims, spread, most, cuts=(), kind=jnp.bfloat16):
    array = jax.random.normal(own_key, dims, jnp.float32) * spread
    if len(cuts) > 0:
        array = level_of(own_key, dims, cuts, -0.22, 0.18) * array
    return jnp.clip(array, min=-most, max=most).astype(kind)


def setup_inputs(seed: int = 0, part: int = 0) -> dict:
    key_list = jax.random.split(jax.random.key(seed), 7)
    part_keys = jax.random.split(jax.random.fold_in(key_list[6], part), 7)
    return {
        "stem_tensor": normal_values(part_keys[0], (2, SWAP_A, SWAP_B, AMPS, LOCAL_R), 1.0, 6.0, ((1, 16),)),
        "branch_one": normal_values(key_list[1], (2, SWAP_A, SWAP_A), (2 * SWAP_A) ** -0.5, 0.1875),
        "branch_two": normal_values(key_list[2], (2, LOCAL_R, LOCAL_R), (2 * LOCAL_R) ** -0.5, 0.25),
        "mode_order": jax.random.permutation(key_list[3], LOCAL_R).astype(jnp.int32),
        "branch_three": normal_values(key_list[4], (2, SWAP_B, SWAP_B), (2 * SWAP_B) ** -0.5, 0.1875),
        "closing": normal_values(key_list[5], (2, SWAP_A, SWAP_B), 0.7, 4.0),
    }


exact_mode = lax.Precision.HIGHEST


def complex_mix(input_real, input_imag, weight_real, weight_imag, pattern):
    def product(first_op, second_op):
        return jnp.einsum(pattern, first_op, second_op, precision=exact_mode)
    return (product(input_real, weight_real) - product(input_imag, weight_imag),
            product(input_real, weight_imag) + product(input_imag, weight_real))


def front_block(block_in, close_block, weights_one, weights_two, mode_order):
    values = block_in.astype(jnp.float32)
    real_part, imag_part = complex_mix(values[0], values[1], weights_one[0], weights_one[1], "abkr,ac->cbkr")
    close_real = close_block[0][:, :, None, None]
    close_imag = close_block[1][:, :, None, None]
    phased = jnp.stack([close_real * real_part - close_imag * imag_part,
                        close_real * imag_part + close_imag * real_part]).astype(jnp.bfloat16)
    reordered = phased.astype(jnp.float32)[..., mode_order]
    real_two, imag_two = complex_mix(reordered[0], reordered[1], weights_two[0], weights_two[1], "abkr,rq->abkq")
    return jnp.stack([real_two, imag_two]).astype(jnp.bfloat16)


def reference(stem_tensor, branch_one, branch_two, mode_order, branch_three, closing):
    weights_one = branch_one.astype(jnp.float32)
    weights_two = branch_two.astype(jnp.float32)
    weights_three = branch_three.astype(jnp.float32)
    close_all = closing.astype(jnp.float32)
    block_cols = 64
    col_blocks = SWAP_B // block_cols

    def front_step(block_index):
        block_in = lax.dynamic_slice_in_dim(stem_tensor, block_index * block_cols, block_cols, 2)
        close_block = lax.dynamic_slice_in_dim(close_all, block_index * block_cols, block_cols, 2)
        return front_block(block_in, close_block, weights_one, weights_two, mode_order)

    pieces = lax.map(front_step, jnp.arange(col_blocks, dtype=jnp.int32))
    second = jnp.moveaxis(pieces, 0, 2).reshape(2, SWAP_A, SWAP_B, AMPS, LOCAL_R)
    block_rows = 16

    def closing_step(block_index):
        row_block = lax.dynamic_slice_in_dim(second, block_index * block_rows, block_rows, 1).astype(jnp.float32)
        out_real, out_imag = complex_mix(row_block[0], row_block[1], weights_three[0], weights_three[1], "abkr,bc->ackr")
        return jnp.stack([out_real, out_imag], axis=2)

    blocks = lax.map(closing_step, jnp.arange(SWAP_A // block_rows, dtype=jnp.int32))
    return blocks.reshape(SWAP_A, SWAP_B, 2, AMPS, LOCAL_R)
```

```python
import functools

import jax
import jax.numpy as jnp
from jax import lax
from jax.experimental import pallas as pl
from jax.experimental.pallas import tpu as pltpu
from jax.sharding import PartitionSpec as P

MESH = pl.DeviceIdType.MESH
CHUNKS = 2


def complex_mix(input_real, input_imag, weight_real, weight_imag, pattern):

    def product(first_op, second_op):
        return jnp.einsum(pattern, first_op, second_op, preferred_element_type=jnp.float32)

    return (
        product(input_real, weight_real) - product(input_imag, weight_imag),
        product(input_real, weight_imag) + product(input_imag, weight_real),
    )


def plain_device(stem_tensor, branch_one, branch_two, mode_order, branch_three, closing):
    group_size = lax.axis_size("inter")
    my_index = lax.axis_index("inter")
    local_b = branch_three.shape[1] // group_size
    permuted = jnp.zeros_like(branch_two).at[:, mode_order, :].set(branch_two)
    close_cols = lax.dynamic_slice_in_dim(closing, my_index * local_b, local_b, 2).astype(
        jnp.float32
    )
    close_real = close_cols[0][:, :, None, None]
    close_imag = close_cols[1][:, :, None, None]
    received = lax.all_to_all(stem_tensor, "inter", split_axis=2, concat_axis=1, tiled=True)
    real_part, imag_part = complex_mix(
        received[0], received[1], branch_one[0], branch_one[1], "abkr,ac->cbkr"
    )
    phased = jnp.stack(
        [
            close_real * real_part - close_imag * imag_part,
            close_real * imag_part + close_imag * real_part,
        ]
    ).astype(jnp.bfloat16)
    real_two, imag_two = complex_mix(
        phased[0], phased[1], permuted[0], permuted[1], "abkr,rq->abkq"
    )
    second = jnp.stack([real_two, imag_two]).astype(jnp.bfloat16)
    returned = lax.all_to_all(second, "inter", split_axis=1, concat_axis=2, tiled=True)
    out_real, out_imag = complex_mix(
        returned[0], returned[1], branch_three[0], branch_three[1], "abkr,bc->ackr"
    )
    return jnp.stack([out_real, out_imag], axis=2)


def swap_kernel(
    n, stem, w_one, w_two, close_ref, to_b, to_a, returned,
    held, turned, out_send, out_recv, back_send, back_recv, own_sem,
):
    me = lax.axis_index("inter")
    la = stem.shape[1]
    chunks, _, size_a, cb, size_r = held.shape
    lb = chunks * cb

    def rows(d):
        return pl.ds(pl.multiple_of(d * la, la), la)

    def peer(i):
        return lax.rem(me + i, n)

    def away(k, i):
        d = peer(i)
        return pltpu.make_async_remote_copy(
            src_ref=stem.at[:, :, pl.ds(pl.multiple_of(d * lb + k * cb, cb), cb), :],
            dst_ref=held.at[k, :, rows(me)],
            send_sem=out_send.at[k, i],
            recv_sem=out_recv.at[k, me],
            device_id={"inter": d},
            device_id_type=MESH,
        )

    def arrival(k, s):
        return pltpu.make_async_remote_copy(
            src_ref=stem.at[:, :, pl.ds(k * cb, cb), :],
            dst_ref=held.at[k, :, rows(s)],
            send_sem=out_send.at[k, 0],
            recv_sem=out_recv.at[k, s],
            device_id={"inter": s},
            device_id_type=MESH,
        )

    def own_in(k):
        return pltpu.make_async_copy(
            stem.at[:, :, pl.ds(pl.multiple_of(me * lb + k * cb, cb), cb), :],
            held.at[k, :, rows(me)],
            own_sem.at[0, k],
        )

    def back(k, i):
        d = peer(i)
        return pltpu.make_async_remote_copy(
            src_ref=held.at[k, :, rows(d)],
            dst_ref=returned.at[:, :, pl.ds(pl.multiple_of(me * lb + k * cb, cb), cb), :],
            send_sem=back_send.at[k, i],
            recv_sem=back_recv.at[k, me],
            device_id={"inter": d},
            device_id_type=MESH,
        )

    def back_arrival(k, s):
        return pltpu.make_async_remote_copy(
            src_ref=held.at[k, :, rows(s)],
            dst_ref=returned.at[:, :, pl.ds(pl.multiple_of(s * lb + k * cb, cb), cb), :],
            send_sem=back_send.at[k, 0],
            recv_sem=back_recv.at[k, s],
            device_id={"inter": s},
            device_id_type=MESH,
        )

    def own_back(k):
        return pltpu.make_async_copy(
            held.at[k, :, rows(me)],
            returned.at[:, :, pl.ds(pl.multiple_of(me * lb + k * cb, cb), cb), :],
            own_sem.at[1, k],
        )

    barrier = pltpu.get_barrier_semaphore()

    @pl.loop(1, n)
    def _(i):
        pl.semaphore_signal(barrier, inc=1, device_id={"inter": peer(i)}, device_id_type=MESH)

    pl.semaphore_wait(barrier, n - 1)

    @pl.loop(1, n)
    def _(i):
        away(0, i).start()

    for k in range(chunks):
        own_in(k).start()

    for k in range(1, chunks):
        @pl.loop(1, n)
        def _(i):
            away(k - 1, i).wait_send()
            away(k, i).start()

    for k in range(chunks):
        own_in(k).wait()

        def turn(s):
            for p in range(2):
                block = held[k, p, rows(s)].reshape(la * cb, size_r)
                moved = jnp.dot(to_b[...], block, preferred_element_type=jnp.float32)
                turned[:, pl.ds(pl.multiple_of(p * size_a + s * la, la), la), :] = (
                    moved.astype(jnp.bfloat16).reshape(cb, la, size_r)
                )

        turn(me)

        @pl.loop(1, n)
        def _(i):
            s = peer(i)
            arrival(k, s).wait_recv()
            turn(s)

        @pl.loop(0, cb)
        def _(b):
            mixed = jnp.dot(w_one[...], turned[b], preferred_element_type=jnp.float32)
            hot = lax.broadcasted_iota(jnp.int32, (close_ref.shape[1], size_r), 0) == k * cb + b
            gate = jnp.dot(
                close_ref[...],
                jnp.where(hot, 1.0, 0.0).astype(jnp.bfloat16),
                preferred_element_type=jnp.float32,
            )
            real_part, imag_part = mixed[:size_a], mixed[size_a:]
            gate_real, gate_imag = gate[:size_a], gate[size_a:]
            phased = jnp.concatenate(
                [
                    (gate_real * real_part - gate_imag * imag_part).astype(jnp.bfloat16),
                    (gate_real * imag_part + gate_imag * real_part).astype(jnp.bfloat16),
                ],
                axis=1,
            )
            both = jnp.dot(phased, w_two[...], preferred_element_type=jnp.float32).astype(
                jnp.bfloat16
            )
            turned[b, :size_a] = both[:, :size_r]
            turned[b, size_a:] = both[:, size_r:]

        def unturn(d):
            for p in range(2):
                block = turned[
                    :, pl.ds(pl.multiple_of(p * size_a + d * la, la), la), :
                ].reshape(cb * la, size_r)
                moved = jnp.dot(to_a[...], block, preferred_element_type=jnp.float32)
                held[k, p, rows(d)] = moved.astype(jnp.bfloat16).reshape(la, cb, size_r)

        @pl.loop(1, n)
        def _(i):
            unturn(peer(i))
            back(k, i).start()

        unturn(me)
        own_back(k).start()

    @pl.loop(1, n)
    def _(i):
        away(chunks - 1, i).wait_send()

    for k in range(chunks):
        own_back(k).wait()

        @pl.loop(1, n)
        def _(i):
            back(k, i).wait_send()
            back_arrival(k, peer(i)).wait_recv()


def close_kernel(block_ref, w_three, out_ref):
    two, _, size_b, size_q = block_ref.shape
    half = size_q // 2
    block = block_ref[:, 0].reshape(two * size_b, size_q)
    mixed = jnp.dot(w_three[...], block, preferred_element_type=jnp.float32)
    groups = mixed.shape[0] // 8
    left = mixed[:, :half].reshape(groups, 8, half)
    right = mixed[:, half:].reshape(groups, 8, half)
    even = lax.broadcasted_iota(jnp.int32, left.shape, 1) % 2 == 0
    low = jnp.where(even, left, pltpu.roll(right, 1, 1))
    high = jnp.where(even, pltpu.roll(left, 7, 1), right)
    out_ref[:, 0] = low
    out_ref[:, 1] = high


def kernel_device(stem_tensor, branch_one, branch_two, mode_order, branch_three, closing):
    n = lax.axis_size("inter")
    me = lax.axis_index("inter")
    _, la, size_b, _, size_r = stem_tensor.shape
    size_a = branch_one.shape[1]
    size_c = branch_three.shape[2]
    lb = size_b // n
    cb = lb // CHUNKS
    stem = stem_tensor.reshape(2, la, size_b, size_r)

    one_t = jnp.swapaxes(branch_one, 1, 2)
    w_one = jnp.concatenate(
        [
            jnp.concatenate([one_t[0], -one_t[1]], axis=1),
            jnp.concatenate([one_t[1], one_t[0]], axis=1),
        ],
        axis=0,
    )
    places = (jnp.arange(size_r, dtype=jnp.int32)[:, None] == mode_order[None, :]).astype(
        jnp.bfloat16
    )
    permuted = jnp.einsum(
        "ir,prq->piq", places, branch_two, preferred_element_type=jnp.float32
    ).astype(jnp.bfloat16)
    w_two = jnp.concatenate(
        [
            jnp.concatenate([permuted[0], permuted[1]], axis=1),
            jnp.concatenate([-permuted[1], permuted[0]], axis=1),
        ],
        axis=0,
    )
    close_cols = lax.dynamic_slice_in_dim(closing, me * lb, lb, 2).reshape(2 * size_a, lb)
    close_cols = jnp.pad(close_cols, ((0, 0), (0, -lb % 128)))
    line = jnp.arange(la * cb, dtype=jnp.int32)
    to_b = ((line // la)[:, None] == (line % cb)[None, :]) & (
        (line % la)[:, None] == (line // cb)[None, :]
    )
    to_b = to_b.astype(jnp.bfloat16)
    to_a = to_b.T

    vmem = pl.BlockSpec(memory_space=pltpu.VMEM)
    anywhere = pl.BlockSpec(memory_space=pl.ANY)
    returned = pl.pallas_call(
        functools.partial(swap_kernel, n),
        out_shape=jax.ShapeDtypeStruct((2, la, size_b, size_r), jnp.bfloat16),
        in_specs=[anywhere, vmem, vmem, vmem, vmem, vmem],
        out_specs=anywhere,
        scratch_shapes=[
            pltpu.VMEM((CHUNKS, 2, size_a, cb, size_r), jnp.bfloat16),
            pltpu.VMEM((cb, 2 * size_a, size_r), jnp.bfloat16),
            pltpu.SemaphoreType.DMA((CHUNKS, n)),
            pltpu.SemaphoreType.DMA((CHUNKS, n)),
            pltpu.SemaphoreType.DMA((CHUNKS, n)),
            pltpu.SemaphoreType.DMA((CHUNKS, n)),
            pltpu.SemaphoreType.DMA((2, CHUNKS)),
        ],
        compiler_params=pltpu.CompilerParams(
            collective_id=0, has_side_effects=True, vmem_limit_bytes=52 * 1024 * 1024
        ),
        cost_estimate=pl.CostEstimate(
            flops=24 * size_a * size_a * lb * size_r,
            bytes_accessed=16 * size_a * lb * size_r,
            transcendentals=0,
        ),
    )(stem, w_one, w_two, close_cols, to_b, to_a)

    three_t = jnp.swapaxes(branch_three, 1, 2)
    w_three = jnp.stack(
        [
            jnp.concatenate([three_t[0], -three_t[1]], axis=1),
            jnp.concatenate([three_t[1], three_t[0]], axis=1),
        ],
        axis=1,
    )
    w_three = (
        w_three.reshape(size_c // 4, 2, 2, 2, 2 * size_b)
        .transpose(0, 2, 3, 1, 4)
        .reshape(2 * size_c, 2 * size_b)
    )
    groups = size_c // 4
    half = size_r // 2
    out = pl.pallas_call(
        close_kernel,
        grid=(la,),
        out_shape=jax.ShapeDtypeStruct((la * groups, 2, 8, half), jnp.float32),
        in_specs=[
            pl.BlockSpec((2, 1, size_b, size_r), lambda a: (0, a, 0, 0)),
            pl.BlockSpec((2 * size_c, 2 * size_b), lambda a: (0, 0)),
        ],
        out_specs=pl.BlockSpec((groups, 2, 8, half), lambda a: (a, 0, 0, 0)),
        compiler_params=pltpu.CompilerParams(vmem_limit_bytes=56 * 1024 * 1024),
        cost_estimate=pl.CostEstimate(
            flops=8 * la * size_b * size_c * size_r,
            bytes_accessed=la * (4 * size_b + 8 * size_c) * size_r,
            transcendentals=0,
        ),
    )(returned, w_three)
    return out.reshape(la, size_c, 2, 1, size_r)


def on_device(stem_tensor, branch_one, branch_two, mode_order, branch_three, closing):
    n = lax.axis_size("inter")
    _, la, size_b, amps, size_r = stem_tensor.shape
    lb = size_b // n
    fits = (
        amps == 1
        and n > 1
        and la % 16 == 0
        and lb % (16 * CHUNKS) == 0
        and size_r == 256
        and branch_one.shape[1] % 16 == 0
        and branch_three.shape[2] % 4 == 0
    )
    device = kernel_device if fits else plain_device
    return device(stem_tensor, branch_one, branch_two, mode_order, branch_three, closing)


def solution(mesh):
    in_specs = (P(None, ("cuts", "inter"), None, None, None), P(), P(), P(), P(), P())
    out_specs = P(("cuts", "inter"), None, None, None, None)
    return jax.shard_map(
        on_device, mesh=mesh, in_specs=in_specs, out_specs=out_specs, check_vma=False
    )
```

```python
import functools

import jax
import jax.numpy as jnp
import numpy as np
from jax import lax
from jax.experimental import pallas as pl
from jax.experimental.pallas import tpu as pltpu
from jax.sharding import PartitionSpec as P

MESH = pl.DeviceIdType.MESH
CHUNKS = 2
RUN = 64


def complex_mix(input_real, input_imag, weight_real, weight_imag, pattern):

    def product(first_op, second_op):
        return jnp.einsum(pattern, first_op, second_op, preferred_element_type=jnp.float32)

    return (
        product(input_real, weight_real) - product(input_imag, weight_imag),
        product(input_real, weight_imag) + product(input_imag, weight_real),
    )


def plain_device(stem_tensor, branch_one, branch_two, mode_order, branch_three, closing):
    group_size = lax.axis_size("inter")
    my_index = lax.axis_index("inter")
    local_b = branch_three.shape[1] // group_size
    permuted = jnp.zeros_like(branch_two).at[:, mode_order, :].set(branch_two)
    close_cols = lax.dynamic_slice_in_dim(closing, my_index * local_b, local_b, 2).astype(
        jnp.float32
    )
    close_real = close_cols[0][:, :, None, None]
    close_imag = close_cols[1][:, :, None, None]
    received = lax.all_to_all(stem_tensor, "inter", split_axis=2, concat_axis=1, tiled=True)
    real_part, imag_part = complex_mix(
        received[0], received[1], branch_one[0], branch_one[1], "abkr,ac->cbkr"
    )
    phased = jnp.stack(
        [
            close_real * real_part - close_imag * imag_part,
            close_real * imag_part + close_imag * real_part,
        ]
    ).astype(jnp.bfloat16)
    real_two, imag_two = complex_mix(
        phased[0], phased[1], permuted[0], permuted[1], "abkr,rq->abkq"
    )
    second = jnp.stack([real_two, imag_two]).astype(jnp.bfloat16)
    returned = lax.all_to_all(second, "inter", split_axis=1, concat_axis=2, tiled=True)
    out_real, out_imag = complex_mix(
        returned[0], returned[1], branch_three[0], branch_three[1], "abkr,bc->ackr"
    )
    return jnp.stack([out_real, out_imag], axis=2)


def swap_kernel(
    n, stem, branch_one, branch_two, mode_order, branch_three, closing, to_b, to_a, spread,
    returned, w_three,
    held, turned, w_one, w_two, close_ref, stacked, shuffled,
    out_send, out_recv, back_send, back_recv, own_sem,
):
    me = lax.axis_index("inter")
    la = stem.shape[1]
    chunks, _, size_a, cb, size_r = held.shape
    lb = chunks * cb
    stride = 7 if n % 7 else 1

    def rows(d):
        return pl.ds(pl.multiple_of(d * la, la), la)

    def peer(i):
        return lax.rem(me + stride * i, n)

    def columns(d, k):
        return pl.ds(pl.multiple_of(d * lb + k * cb, cb), cb)

    def away(k, i):
        d = peer(i)
        return pltpu.make_async_remote_copy(
            src_ref=stem.at[:, :, columns(d, k), :],
            dst_ref=held.at[k, :, rows(me)],
            send_sem=out_send.at[k, i],
            recv_sem=out_recv.at[k, me],
            device_id={"inter": d},
            device_id_type=MESH,
        )

    def arrival(k, s):
        return pltpu.make_async_remote_copy(
            src_ref=stem.at[:, :, columns(0, k), :],
            dst_ref=held.at[k, :, rows(s)],
            send_sem=out_send.at[k, 0],
            recv_sem=out_recv.at[k, s],
            device_id={"inter": s},
            device_id_type=MESH,
        )

    def own_in(k):
        return pltpu.make_async_copy(
            stem.at[:, :, columns(me, k), :], held.at[k, :, rows(me)], own_sem.at[0, k]
        )

    def back(k, i):
        d = peer(i)
        return pltpu.make_async_remote_copy(
            src_ref=held.at[k, :, rows(d)],
            dst_ref=returned.at[k, me],
            send_sem=back_send.at[k, i],
            recv_sem=back_recv.at[k, me],
            device_id={"inter": d},
            device_id_type=MESH,
        )

    def back_arrival(k, s):
        return pltpu.make_async_remote_copy(
            src_ref=held.at[k, :, rows(s)],
            dst_ref=returned.at[k, s],
            send_sem=back_send.at[k, 0],
            recv_sem=back_recv.at[k, s],
            device_id={"inter": s},
            device_id_type=MESH,
        )

    def own_back(k):
        return pltpu.make_async_copy(
            held.at[k, :, rows(me)], returned.at[k, me], own_sem.at[1, k]
        )

    def weights_out():
        return pltpu.make_async_copy(shuffled, w_three, own_sem.at[2, 0])

    barrier = pltpu.get_barrier_semaphore()

    @pl.loop(1, n)
    def _(i):
        pl.semaphore_signal(barrier, inc=1, device_id={"inter": peer(i)}, device_id_type=MESH)

    pl.semaphore_wait(barrier, n - 1)

    @pl.loop(1, n)
    def _(i):
        away(0, i).start()

    for k in range(chunks):
        own_in(k).start()

    one_real = branch_one[0].astype(jnp.float32).T.astype(jnp.bfloat16)
    one_imag = branch_one[1].astype(jnp.float32).T.astype(jnp.bfloat16)
    w_one[:size_a, :size_a] = one_real
    w_one[:size_a, size_a:] = -one_imag
    w_one[size_a:, :size_a] = one_imag
    w_one[size_a:, size_a:] = one_real

    hot = lax.broadcasted_iota(jnp.int32, (size_r, size_r), 0) == mode_order[...]
    places = jnp.where(hot, 1.0, 0.0).astype(jnp.bfloat16)
    two_real = jnp.dot(places, branch_two[0], preferred_element_type=jnp.float32)
    two_imag = jnp.dot(places, branch_two[1], preferred_element_type=jnp.float32)
    w_two[:size_r, :size_r] = two_real.astype(jnp.bfloat16)
    w_two[:size_r, size_r:] = two_imag.astype(jnp.bfloat16)
    w_two[size_r:, :size_r] = (-two_imag).astype(jnp.bfloat16)
    w_two[size_r:, size_r:] = two_real.astype(jnp.bfloat16)

    pick = (closing.shape[2], close_ref.shape[1])
    picked = lax.broadcasted_iota(jnp.int32, pick, 0) == (
        lax.broadcasted_iota(jnp.int32, pick, 1) + me * lb
    )
    picked = jnp.where(picked, 1.0, 0.0).astype(jnp.bfloat16)
    for p in range(2):
        close_ref[p * size_a : (p + 1) * size_a] = jnp.dot(
            closing[p], picked, preferred_element_type=jnp.float32
        ).astype(jnp.bfloat16)

    width = 2 * n * cb
    for k in range(chunks):
        for part in range(2):
            pieces = []
            for s in range(n):
                piece = branch_three[:, s * lb + k * cb : s * lb + (k + 1) * cb, :].astype(
                    jnp.float32
                )
                pieces += [piece[0], -piece[1]] if part == 0 else [piece[1], piece[0]]
            stacked[part, :, k * width : (k + 1) * width] = (
                jnp.concatenate(pieces, axis=0).T.astype(jnp.bfloat16)
            )
    run = spread.shape[0] // 2
    for t in range(stacked.shape[1] // run):
        block = jnp.concatenate(
            [stacked[0, t * run : (t + 1) * run], stacked[1, t * run : (t + 1) * run]], axis=0
        )
        shuffled[2 * t * run : 2 * (t + 1) * run] = jnp.dot(
            spread[...], block, preferred_element_type=jnp.float32
        ).astype(jnp.bfloat16)
    weights_out().start()

    for k in range(1, chunks):
        @pl.loop(1, n)
        def _(i):
            away(k - 1, i).wait_send()
            away(k, i).start()

    for k in range(chunks):
        own_in(k).wait()

        def turn(s):
            for p in range(2):
                block = held[k, p, rows(s)].reshape(la * cb, size_r)
                moved = jnp.dot(to_b[...], block, preferred_element_type=jnp.float32)
                turned[:, pl.ds(pl.multiple_of(p * size_a + s * la, la), la), :] = (
                    moved.astype(jnp.bfloat16).reshape(cb, la, size_r)
                )

        turn(me)

        @pl.loop(1, n)
        def _(i):
            s = peer(n - i)
            arrival(k, s).wait_recv()
            turn(s)

        @pl.loop(0, cb)
        def _(b):
            mixed = jnp.dot(w_one[...], turned[b], preferred_element_type=jnp.float32)
            hot = lax.broadcasted_iota(jnp.int32, (close_ref.shape[1], size_r), 0) == k * cb + b
            gate = jnp.dot(
                close_ref[...],
                jnp.where(hot, 1.0, 0.0).astype(jnp.bfloat16),
                preferred_element_type=jnp.float32,
            )
            real_part, imag_part = mixed[:size_a], mixed[size_a:]
            gate_real, gate_imag = gate[:size_a], gate[size_a:]
            phased = jnp.concatenate(
                [
                    (gate_real * real_part - gate_imag * imag_part).astype(jnp.bfloat16),
                    (gate_real * imag_part + gate_imag * real_part).astype(jnp.bfloat16),
                ],
                axis=1,
            )
            both = jnp.dot(phased, w_two[...], preferred_element_type=jnp.float32).astype(
                jnp.bfloat16
            )
            turned[b, :size_a] = both[:, :size_r]
            turned[b, size_a:] = both[:, size_r:]

        def unturn(d):
            for p in range(2):
                block = turned[
                    :, pl.ds(pl.multiple_of(p * size_a + d * la, la), la), :
                ].reshape(cb * la, size_r)
                moved = jnp.dot(to_a[...], block, preferred_element_type=jnp.float32)
                held[k, p, rows(d)] = moved.astype(jnp.bfloat16).reshape(la, cb, size_r)

        @pl.loop(1, n)
        def _(i):
            unturn(peer(i))
            if k + 1 < chunks:
                away(k + 1, i).wait_send()
            back(k, i).start()

        unturn(me)
        own_back(k).start()

    weights_out().wait()
    for k in range(chunks):
        own_back(k).wait()

        @pl.loop(1, n)
        def _(i):
            back(k, i).wait_send()
            back_arrival(k, peer(n - i)).wait_recv()


def close_kernel(block_ref, w_three, out_ref):
    chunks, n, two, steps, cb, size_q = block_ref.shape
    half = size_q // 2
    groups = out_ref.shape[0] // steps
    for a in range(steps):
        block = block_ref[:, :, :, a].reshape(chunks * n * two * cb, size_q)
        mixed = jnp.dot(w_three[...], block, preferred_element_type=jnp.float32)
        left = mixed[:, :half].reshape(groups, 8, half)
        right = mixed[:, half:].reshape(groups, 8, half)
        even = lax.broadcasted_iota(jnp.int32, left.shape, 1) % 2 == 0
        own = pl.ds(a * groups, groups)
        out_ref[own, 0] = jnp.where(even, left, pltpu.roll(right, 1, 1))
        out_ref[own, 1] = jnp.where(even, pltpu.roll(left, 7, 1), right)


def kernel_device(stem_tensor, branch_one, branch_two, mode_order, branch_three, closing):
    n = lax.axis_size("inter")
    _, la, size_b, _, size_r = stem_tensor.shape
    size_a = branch_one.shape[1]
    size_c = branch_three.shape[2]
    lb = size_b // n
    cb = lb // CHUNKS
    stem = stem_tensor.reshape(2, la, size_b, size_r)

    line = np.arange(la * cb)
    to_b = (
        ((line // la)[:, None] == (line % cb)[None, :])
        & ((line % la)[:, None] == (line // cb)[None, :])
    ).astype(np.float32)
    g, low, part, high = np.unravel_index(np.arange(2 * RUN), (RUN // 4, 2, 2, 2))
    spread = np.zeros((2 * RUN, 2 * RUN), np.float32)
    spread[np.arange(2 * RUN), part * RUN + 4 * g + 2 * high + low] = 1.0
    to_b, to_a, spread = (jnp.asarray(x, jnp.bfloat16) for x in (to_b, to_b.T, spread))

    vmem = pl.BlockSpec(memory_space=pltpu.VMEM)
    anywhere = pl.BlockSpec(memory_space=pl.ANY)
    returned, w_three = pl.pallas_call(
        functools.partial(swap_kernel, n),
        out_shape=[
            jax.ShapeDtypeStruct((CHUNKS, n, 2, la, cb, size_r), jnp.bfloat16),
            jax.ShapeDtypeStruct((2 * size_c, 2 * size_b), jnp.bfloat16),
        ],
        in_specs=[anywhere] + [vmem] * 8,
        out_specs=[anywhere, anywhere],
        scratch_shapes=[
            pltpu.VMEM((CHUNKS, 2, size_a, cb, size_r), jnp.bfloat16),
            pltpu.VMEM((cb, 2 * size_a, size_r), jnp.bfloat16),
            pltpu.VMEM((2 * size_a, 2 * size_a), jnp.bfloat16),
            pltpu.VMEM((2 * size_r, 2 * size_r), jnp.bfloat16),
            pltpu.VMEM((2 * size_a, pl.cdiv(lb, 128) * 128), jnp.bfloat16),
            pltpu.VMEM((2, size_c, 2 * size_b), jnp.bfloat16),
            pltpu.VMEM((2 * size_c, 2 * size_b), jnp.bfloat16),
            pltpu.SemaphoreType.DMA((CHUNKS, n)),
            pltpu.SemaphoreType.DMA((CHUNKS, n)),
            pltpu.SemaphoreType.DMA((CHUNKS, n)),
            pltpu.SemaphoreType.DMA((CHUNKS, n)),
            pltpu.SemaphoreType.DMA((3, CHUNKS)),
        ],
        compiler_params=pltpu.CompilerParams(
            collective_id=0, has_side_effects=True, vmem_limit_bytes=56 * 1024 * 1024
        ),
        cost_estimate=pl.CostEstimate(
            flops=24 * size_a * size_a * lb * size_r,
            bytes_accessed=16 * size_a * lb * size_r,
            transcendentals=0,
        ),
    )(
        stem, branch_one, branch_two, mode_order.reshape(1, size_r), branch_three, closing,
        to_b, to_a, spread,
    )

    groups = size_c // 4
    half = size_r // 2
    steps = 4
    out = pl.pallas_call(
        close_kernel,
        grid=(la // steps,),
        out_shape=jax.ShapeDtypeStruct((la * groups, 2, 8, half), jnp.float32),
        in_specs=[
            pl.BlockSpec((CHUNKS, n, 2, steps, cb, size_r), lambda a: (0, 0, 0, a, 0, 0)),
            pl.BlockSpec((2 * size_c, 2 * size_b), lambda a: (0, 0)),
        ],
        out_specs=pl.BlockSpec((steps * groups, 2, 8, half), lambda a: (a, 0, 0, 0)),
        compiler_params=pltpu.CompilerParams(vmem_limit_bytes=56 * 1024 * 1024),
        cost_estimate=pl.CostEstimate(
            flops=8 * la * size_b * size_c * size_r,
            bytes_accessed=la * (4 * size_b + 8 * size_c) * size_r,
            transcendentals=0,
        ),
    )(returned, w_three)
    return out.reshape(la, size_c, 2, 1, size_r)


def on_device(stem_tensor, branch_one, branch_two, mode_order, branch_three, closing):
    n = lax.axis_size("inter")
    _, la, size_b, amps, size_r = stem_tensor.shape
    lb = size_b // n
    fits = (
        amps == 1
        and n > 1
        and la % 16 == 0
        and lb % (16 * CHUNKS) == 0
        and size_r == 256
        and branch_one.shape[1] % 16 == 0
        and branch_three.shape[2] % RUN == 0
    )
    device = kernel_device if fits else plain_device
    return device(stem_tensor, branch_one, branch_two, mode_order, branch_three, closing)


def solution(mesh):
    in_specs = (P(None, ("cuts", "inter"), None, None, None), P(), P(), P(), P(), P())
    out_specs = P(("cuts", "inter"), None, None, None, None)
    return jax.shard_map(
        on_device, mesh=mesh, in_specs=in_specs, out_specs=out_specs, check_vma=False
    )
```

```python
import functools

import jax
import jax.numpy as jnp
import numpy as np
from jax import lax
from jax.experimental import pallas as pl
from jax.experimental.pallas import tpu as pltpu
from jax.sharding import PartitionSpec as P

MESH = pl.DeviceIdType.MESH
CHUNKS = 2
RUN = 64


def complex_mix(input_real, input_imag, weight_real, weight_imag, pattern):

    def product(first_op, second_op):
        return jnp.einsum(pattern, first_op, second_op, preferred_element_type=jnp.float32)

    return (
        product(input_real, weight_real) - product(input_imag, weight_imag),
        product(input_real, weight_imag) + product(input_imag, weight_real),
    )


def plain_device(stem_tensor, branch_one, branch_two, mode_order, branch_three, closing):
    group_size = lax.axis_size("inter")
    my_index = lax.axis_index("inter")
    local_b = branch_three.shape[1] // group_size
    permuted = jnp.zeros_like(branch_two).at[:, mode_order, :].set(branch_two)
    close_cols = lax.dynamic_slice_in_dim(closing, my_index * local_b, local_b, 2).astype(
        jnp.float32
    )
    close_real = close_cols[0][:, :, None, None]
    close_imag = close_cols[1][:, :, None, None]
    received = lax.all_to_all(stem_tensor, "inter", split_axis=2, concat_axis=1, tiled=True)
    real_part, imag_part = complex_mix(
        received[0], received[1], branch_one[0], branch_one[1], "abkr,ac->cbkr"
    )
    phased = jnp.stack(
        [
            close_real * real_part - close_imag * imag_part,
            close_real * imag_part + close_imag * real_part,
        ]
    ).astype(jnp.bfloat16)
    real_two, imag_two = complex_mix(
        phased[0], phased[1], permuted[0], permuted[1], "abkr,rq->abkq"
    )
    second = jnp.stack([real_two, imag_two]).astype(jnp.bfloat16)
    returned = lax.all_to_all(second, "inter", split_axis=1, concat_axis=2, tiled=True)
    out_real, out_imag = complex_mix(
        returned[0], returned[1], branch_three[0], branch_three[1], "abkr,bc->ackr"
    )
    return jnp.stack([out_real, out_imag], axis=2)


def swap_kernel(
    n, stem, branch_one, branch_two, mode_order, branch_three, closing, to_b, to_a, spread,
    returned, w_three,
    staged, held, turned, w_one, w_two, close_ref, stacked, shuffled,
    stage_sem, out_send, out_recv, back_send, back_recv, own_sem,
):
    me = lax.axis_index("inter")
    la = stem.shape[1]
    chunks, _, size_a, cb, size_r = held.shape
    lb = chunks * cb
    wing = n // 2
    base = me // wing * wing
    other = wing - base

    def rows(d):
        return pl.ds(pl.multiple_of(d * la, la), la)

    def peer(i):
        odd = lax.rem(me, 2)
        turn_odd = lax.rem(i, 2)
        last = jnp.where(i == n - 1, 1, 0)
        crossing = jnp.where(odd == 1, jnp.where(turn_odd == 1, last, 1), turn_odd)
        step_even = (i - crossing) // 2
        step_odd = jnp.where(last == 1, wing - 1, (i + 1) // 2 - crossing)
        step = jnp.where(odd == 1, step_odd, step_even)
        return jnp.where(crossing == 1, other, base) + lax.rem(me + step, wing)

    def columns(d, k):
        return pl.ds(pl.multiple_of(d * lb + k * cb, cb), cb)

    def away(k, i):
        d = peer(i)
        return pltpu.make_async_remote_copy(
            src_ref=staged.at[k, d],
            dst_ref=held.at[k, :, rows(me)],
            send_sem=out_send.at[k, i],
            recv_sem=out_recv.at[k, me],
            device_id={"inter": d},
            device_id_type=MESH,
        )

    def arrival(k, s):
        return pltpu.make_async_remote_copy(
            src_ref=staged.at[k, s],
            dst_ref=held.at[k, :, rows(s)],
            send_sem=out_send.at[k, 0],
            recv_sem=out_recv.at[k, s],
            device_id={"inter": s},
            device_id_type=MESH,
        )

    def stage(k, i):
        d = peer(i)
        return pltpu.make_async_copy(
            stem.at[:, :, columns(d, k), :], staged.at[k, d], stage_sem.at[k, i]
        )

    def own_in(k):
        return pltpu.make_async_copy(
            stem.at[:, :, columns(me, k), :], held.at[k, :, rows(me)], own_sem.at[0, k]
        )

    def back(k, i):
        d = peer(i)
        return pltpu.make_async_remote_copy(
            src_ref=held.at[k, :, rows(d)],
            dst_ref=returned.at[k, me],
            send_sem=back_send.at[k, i],
            recv_sem=back_recv.at[k, me],
            device_id={"inter": d},
            device_id_type=MESH,
        )

    def back_arrival(k, s):
        return pltpu.make_async_remote_copy(
            src_ref=held.at[k, :, rows(s)],
            dst_ref=returned.at[k, s],
            send_sem=back_send.at[k, 0],
            recv_sem=back_recv.at[k, s],
            device_id={"inter": s},
            device_id_type=MESH,
        )

    def own_back(k):
        return pltpu.make_async_copy(
            held.at[k, :, rows(me)], returned.at[k, me], own_sem.at[1, k]
        )

    def weights_out():
        return pltpu.make_async_copy(shuffled, w_three, own_sem.at[2, 0])

    for k in range(chunks):
        @pl.loop(1, n)
        def _(i):
            stage(k, i).start()

    barrier = pltpu.get_barrier_semaphore()

    @pl.loop(1, n)
    def _(i):
        pl.semaphore_signal(barrier, inc=1, device_id={"inter": peer(i)}, device_id_type=MESH)

    pl.semaphore_wait(barrier, n - 1)

    @pl.loop(1, n)
    def _(i):
        stage(0, i).wait()
        away(0, i).start()

    for k in range(chunks):
        own_in(k).start()

    one_real = branch_one[0].astype(jnp.float32).T.astype(jnp.bfloat16)
    one_imag = branch_one[1].astype(jnp.float32).T.astype(jnp.bfloat16)
    w_one[:size_a, :size_a] = one_real
    w_one[:size_a, size_a:] = -one_imag
    w_one[size_a:, :size_a] = one_imag
    w_one[size_a:, size_a:] = one_real

    hot = lax.broadcasted_iota(jnp.int32, (size_r, size_r), 0) == mode_order[...]
    places = jnp.where(hot, 1.0, 0.0).astype(jnp.bfloat16)
    two_real = jnp.dot(places, branch_two[0], preferred_element_type=jnp.float32)
    two_imag = jnp.dot(places, branch_two[1], preferred_element_type=jnp.float32)
    w_two[:size_r, :size_r] = two_real.astype(jnp.bfloat16)
    w_two[:size_r, size_r:] = two_imag.astype(jnp.bfloat16)
    w_two[size_r:, :size_r] = (-two_imag).astype(jnp.bfloat16)
    w_two[size_r:, size_r:] = two_real.astype(jnp.bfloat16)

    pick = (closing.shape[2], close_ref.shape[1])
    picked = lax.broadcasted_iota(jnp.int32, pick, 0) == (
        lax.broadcasted_iota(jnp.int32, pick, 1) + me * lb
    )
    picked = jnp.where(picked, 1.0, 0.0).astype(jnp.bfloat16)
    for p in range(2):
        close_ref[p * size_a : (p + 1) * size_a] = jnp.dot(
            closing[p], picked, preferred_element_type=jnp.float32
        ).astype(jnp.bfloat16)

    width = 2 * n * cb
    for k in range(chunks):
        for part in range(2):
            pieces = []
            for s in range(n):
                piece = branch_three[:, s * lb + k * cb : s * lb + (k + 1) * cb, :].astype(
                    jnp.float32
                )
                pieces += [piece[0], -piece[1]] if part == 0 else [piece[1], piece[0]]
            stacked[part, :, k * width : (k + 1) * width] = (
                jnp.concatenate(pieces, axis=0).T.astype(jnp.bfloat16)
            )
    run = spread.shape[0] // 2
    for t in range(stacked.shape[1] // run):
        block = jnp.concatenate(
            [stacked[0, t * run : (t + 1) * run], stacked[1, t * run : (t + 1) * run]], axis=0
        )
        shuffled[2 * t * run : 2 * (t + 1) * run] = jnp.dot(
            spread[...], block, preferred_element_type=jnp.float32
        ).astype(jnp.bfloat16)
    weights_out().start()

    for k in range(1, chunks):
        @pl.loop(1, n)
        def _(i):
            away(k - 1, i).wait_send()
            stage(k, i).wait()
            away(k, i).start()

    for k in range(chunks):
        own_in(k).wait()

        def turn(s):
            for p in range(2):
                block = held[k, p, rows(s)].reshape(la * cb, size_r)
                moved = jnp.dot(to_b[...], block, preferred_element_type=jnp.float32)
                turned[:, pl.ds(pl.multiple_of(p * size_a + s * la, la), la), :] = (
                    moved.astype(jnp.bfloat16).reshape(cb, la, size_r)
                )

        turn(me)

        @pl.loop(1, n)
        def _(i):
            s = peer(i)
            arrival(k, s).wait_recv()
            turn(s)

        @pl.loop(0, cb)
        def _(b):
            mixed = jnp.dot(w_one[...], turned[b], preferred_element_type=jnp.float32)
            hot = lax.broadcasted_iota(jnp.int32, (close_ref.shape[1], size_r), 0) == k * cb + b
            gate = jnp.dot(
                close_ref[...],
                jnp.where(hot, 1.0, 0.0).astype(jnp.bfloat16),
                preferred_element_type=jnp.float32,
            )
            real_part, imag_part = mixed[:size_a], mixed[size_a:]
            gate_real, gate_imag = gate[:size_a], gate[size_a:]
            phased = jnp.concatenate(
                [
                    (gate_real * real_part - gate_imag * imag_part).astype(jnp.bfloat16),
                    (gate_real * imag_part + gate_imag * real_part).astype(jnp.bfloat16),
                ],
                axis=1,
            )
            both = jnp.dot(phased, w_two[...], preferred_element_type=jnp.float32).astype(
                jnp.bfloat16
            )
            turned[b, :size_a] = both[:, :size_r]
            turned[b, size_a:] = both[:, size_r:]

        def unturn(d):
            for p in range(2):
                block = turned[
                    :, pl.ds(pl.multiple_of(p * size_a + d * la, la), la), :
                ].reshape(cb * la, size_r)
                moved = jnp.dot(to_a[...], block, preferred_element_type=jnp.float32)
                held[k, p, rows(d)] = moved.astype(jnp.bfloat16).reshape(la, cb, size_r)

        @pl.loop(1, n)
        def _(i):
            unturn(peer(i))
            if k + 1 < chunks:
                away(k + 1, i).wait_send()
            back(k, i).start()

        unturn(me)
        own_back(k).start()

    weights_out().wait()
    for k in range(chunks):
        own_back(k).wait()

        @pl.loop(1, n)
        def _(i):
            back(k, i).wait_send()
            back_arrival(k, peer(i)).wait_recv()


def close_kernel(block_ref, w_three, out_ref):
    chunks, n, two, steps, cb, size_q = block_ref.shape
    half = size_q // 2
    groups = out_ref.shape[0] // steps
    for a in range(steps):
        block = block_ref[:, :, :, a].reshape(chunks * n * two * cb, size_q)
        mixed = jnp.dot(w_three[...], block, preferred_element_type=jnp.float32)
        left = mixed[:, :half].reshape(groups, 8, half)
        right = mixed[:, half:].reshape(groups, 8, half)
        even = lax.broadcasted_iota(jnp.int32, left.shape, 1) % 2 == 0
        own = pl.ds(a * groups, groups)
        out_ref[own, 0] = jnp.where(even, left, pltpu.roll(right, 1, 1))
        out_ref[own, 1] = jnp.where(even, pltpu.roll(left, 7, 1), right)


def kernel_device(stem_tensor, branch_one, branch_two, mode_order, branch_three, closing):
    n = lax.axis_size("inter")
    _, la, size_b, _, size_r = stem_tensor.shape
    size_a = branch_one.shape[1]
    size_c = branch_three.shape[2]
    lb = size_b // n
    cb = lb // CHUNKS
    stem = stem_tensor.reshape(2, la, size_b, size_r)

    line = np.arange(la * cb)
    to_b = (
        ((line // la)[:, None] == (line % cb)[None, :])
        & ((line % la)[:, None] == (line // cb)[None, :])
    ).astype(np.float32)
    g, low, part, high = np.unravel_index(np.arange(2 * RUN), (RUN // 4, 2, 2, 2))
    spread = np.zeros((2 * RUN, 2 * RUN), np.float32)
    spread[np.arange(2 * RUN), part * RUN + 4 * g + 2 * high + low] = 1.0
    to_b, to_a, spread = (jnp.asarray(x, jnp.bfloat16) for x in (to_b, to_b.T, spread))

    vmem = pl.BlockSpec(memory_space=pltpu.VMEM)
    anywhere = pl.BlockSpec(memory_space=pl.ANY)
    returned, w_three = pl.pallas_call(
        functools.partial(swap_kernel, n),
        out_shape=[
            jax.ShapeDtypeStruct((CHUNKS, n, 2, la, cb, size_r), jnp.bfloat16),
            jax.ShapeDtypeStruct((2 * size_c, 2 * size_b), jnp.bfloat16),
        ],
        in_specs=[anywhere] + [vmem] * 8,
        out_specs=[anywhere, anywhere],
        scratch_shapes=[
            pltpu.VMEM((CHUNKS, n, 2, la, cb, size_r), jnp.bfloat16),
            pltpu.VMEM((CHUNKS, 2, size_a, cb, size_r), jnp.bfloat16),
            pltpu.VMEM((cb, 2 * size_a, size_r), jnp.bfloat16),
            pltpu.VMEM((2 * size_a, 2 * size_a), jnp.bfloat16),
            pltpu.VMEM((2 * size_r, 2 * size_r), jnp.bfloat16),
            pltpu.VMEM((2 * size_a, pl.cdiv(lb, 128) * 128), jnp.bfloat16),
            pltpu.VMEM((2, size_c, 2 * size_b), jnp.bfloat16),
            pltpu.VMEM((2 * size_c, 2 * size_b), jnp.bfloat16),
            pltpu.SemaphoreType.DMA((CHUNKS, n)),
            pltpu.SemaphoreType.DMA((CHUNKS, n)),
            pltpu.SemaphoreType.DMA((CHUNKS, n)),
            pltpu.SemaphoreType.DMA((CHUNKS, n)),
            pltpu.SemaphoreType.DMA((CHUNKS, n)),
            pltpu.SemaphoreType.DMA((3, CHUNKS)),
        ],
        compiler_params=pltpu.CompilerParams(
            collective_id=0, has_side_effects=True, vmem_limit_bytes=62 * 1024 * 1024
        ),
        cost_estimate=pl.CostEstimate(
            flops=24 * size_a * size_a * lb * size_r,
            bytes_accessed=16 * size_a * lb * size_r,
            transcendentals=0,
        ),
    )(
        stem, branch_one, branch_two, mode_order.reshape(1, size_r), branch_three, closing,
        to_b, to_a, spread,
    )

    groups = size_c // 4
    half = size_r // 2
    steps = 4
    out = pl.pallas_call(
        close_kernel,
        grid=(la // steps,),
        out_shape=jax.ShapeDtypeStruct((la * groups, 2, 8, half), jnp.float32),
        in_specs=[
            pl.BlockSpec((CHUNKS, n, 2, steps, cb, size_r), lambda a: (0, 0, 0, a, 0, 0)),
            pl.BlockSpec((2 * size_c, 2 * size_b), lambda a: (0, 0)),
        ],
        out_specs=pl.BlockSpec((steps * groups, 2, 8, half), lambda a: (a, 0, 0, 0)),
        compiler_params=pltpu.CompilerParams(vmem_limit_bytes=56 * 1024 * 1024),
        cost_estimate=pl.CostEstimate(
            flops=8 * la * size_b * size_c * size_r,
            bytes_accessed=la * (4 * size_b + 8 * size_c) * size_r,
            transcendentals=0,
        ),
    )(returned, w_three)
    return out.reshape(la, size_c, 2, 1, size_r)


def on_device(stem_tensor, branch_one, branch_two, mode_order, branch_three, closing):
    n = lax.axis_size("inter")
    _, la, size_b, amps, size_r = stem_tensor.shape
    lb = size_b // n
    fits = (
        amps == 1
        and n % 2 == 0
        and la % 16 == 0
        and lb % (16 * CHUNKS) == 0
        and size_r == 256
        and branch_one.shape[1] % 16 == 0
        and branch_three.shape[2] % RUN == 0
    )
    device = kernel_device if fits else plain_device
    return device(stem_tensor, branch_one, branch_two, mode_order, branch_three, closing)


def solution(mesh):
    in_specs = (P(None, ("cuts", "inter"), None, None, None), P(), P(), P(), P(), P())
    out_specs = P(("cuts", "inter"), None, None, None, None)
    return jax.shard_map(
        on_device, mesh=mesh, in_specs=in_specs, out_specs=out_specs, check_vma=False
    )
```

```python
import functools

import jax
import jax.numpy as jnp
import numpy as np
from jax import lax
from jax.experimental import pallas as pl
from jax.experimental.pallas import tpu as pltpu
from jax.sharding import PartitionSpec as P

MESH = pl.DeviceIdType.MESH
CHUNKS = 2
WINDOW = 4
RUN = 64


def complex_mix(input_real, input_imag, weight_real, weight_imag, pattern):

    def product(first_op, second_op):
        return jnp.einsum(pattern, first_op, second_op, preferred_element_type=jnp.float32)

    return (
        product(input_real, weight_real) - product(input_imag, weight_imag),
        product(input_real, weight_imag) + product(input_imag, weight_real),
    )


def plain_device(stem_tensor, branch_one, branch_two, mode_order, branch_three, closing):
    group_size = lax.axis_size("inter")
    my_index = lax.axis_index("inter")
    local_b = branch_three.shape[1] // group_size
    permuted = jnp.zeros_like(branch_two).at[:, mode_order, :].set(branch_two)
    close_cols = lax.dynamic_slice_in_dim(closing, my_index * local_b, local_b, 2).astype(
        jnp.float32
    )
    close_real = close_cols[0][:, :, None, None]
    close_imag = close_cols[1][:, :, None, None]
    received = lax.all_to_all(stem_tensor, "inter", split_axis=2, concat_axis=1, tiled=True)
    real_part, imag_part = complex_mix(
        received[0], received[1], branch_one[0], branch_one[1], "abkr,ac->cbkr"
    )
    phased = jnp.stack(
        [
            close_real * real_part - close_imag * imag_part,
            close_real * imag_part + close_imag * real_part,
        ]
    ).astype(jnp.bfloat16)
    real_two, imag_two = complex_mix(
        phased[0], phased[1], permuted[0], permuted[1], "abkr,rq->abkq"
    )
    second = jnp.stack([real_two, imag_two]).astype(jnp.bfloat16)
    returned = lax.all_to_all(second, "inter", split_axis=1, concat_axis=2, tiled=True)
    out_real, out_imag = complex_mix(
        returned[0], returned[1], branch_three[0], branch_three[1], "abkr,bc->ackr"
    )
    return jnp.stack([out_real, out_imag], axis=2)


def swap_kernel(
    n, stem, branch_one, branch_two, mode_order, branch_three, closing, to_b, to_a, spread,
    returned, w_three,
    staged, held, turned, w_one, w_two, close_ref, stacked, shuffled,
    stage_sem, out_send, out_recv, back_send, back_recv, own_sem,
):
    me = lax.axis_index("inter")
    la = stem.shape[1]
    chunks, _, size_a, cb, size_r = held.shape
    lb = chunks * cb
    window = min(WINDOW, n - 1)
    wing = n // 2
    base = me // wing * wing
    other = wing - base

    def rows(d):
        return pl.ds(pl.multiple_of(d * la, la), la)

    def peer(i):
        odd = lax.rem(me, 2)
        turn_odd = lax.rem(i, 2)
        last = jnp.where(i == n - 1, 1, 0)
        crossing = jnp.where(odd == 1, jnp.where(turn_odd == 1, last, 1), turn_odd)
        step_even = (i - crossing) // 2
        step_odd = jnp.where(last == 1, wing - 1, (i + 1) // 2 - crossing)
        step = jnp.where(odd == 1, step_odd, step_even)
        return jnp.where(crossing == 1, other, base) + lax.rem(me + step, wing)

    def columns(d, k):
        return pl.ds(pl.multiple_of(d * lb + k * cb, cb), cb)

    def away(k, i):
        d = peer(i)
        return pltpu.make_async_remote_copy(
            src_ref=staged.at[k, d],
            dst_ref=held.at[k, :, rows(me)],
            send_sem=out_send.at[k, i],
            recv_sem=out_recv.at[k, me],
            device_id={"inter": d},
            device_id_type=MESH,
        )

    def arrival(k, s):
        return pltpu.make_async_remote_copy(
            src_ref=staged.at[k, s],
            dst_ref=held.at[k, :, rows(s)],
            send_sem=out_send.at[k, 0],
            recv_sem=out_recv.at[k, s],
            device_id={"inter": s},
            device_id_type=MESH,
        )

    def stage(k, i):
        d = peer(i)
        return pltpu.make_async_copy(
            stem.at[:, :, columns(d, k), :], staged.at[k, d], stage_sem.at[k, i]
        )

    def own_in(k):
        return pltpu.make_async_copy(
            stem.at[:, :, columns(me, k), :], held.at[k, :, rows(me)], own_sem.at[0, k]
        )

    def back(k, i):
        d = peer(i)
        return pltpu.make_async_remote_copy(
            src_ref=held.at[k, :, rows(d)],
            dst_ref=returned.at[k, me],
            send_sem=back_send.at[k, i],
            recv_sem=back_recv.at[k, me],
            device_id={"inter": d},
            device_id_type=MESH,
        )

    def back_arrival(k, s):
        return pltpu.make_async_remote_copy(
            src_ref=held.at[k, :, rows(s)],
            dst_ref=returned.at[k, s],
            send_sem=back_send.at[k, 0],
            recv_sem=back_recv.at[k, s],
            device_id={"inter": s},
            device_id_type=MESH,
        )

    def own_back(k):
        return pltpu.make_async_copy(
            held.at[k, :, rows(me)], returned.at[k, me], own_sem.at[1, k]
        )

    def weights_out():
        return pltpu.make_async_copy(shuffled, w_three, own_sem.at[2, 0])

    for k in range(chunks):
        @pl.loop(1, n)
        def _(i):
            stage(k, i).start()

    barrier = pltpu.get_barrier_semaphore()

    @pl.loop(1, n)
    def _(i):
        pl.semaphore_signal(barrier, inc=1, device_id={"inter": peer(i)}, device_id_type=MESH)

    pl.semaphore_wait(barrier, n - 1)

    @pl.loop(1, n)
    def _(i):
        stage(0, i).wait()

        @pl.when(i > window)
        def _():
            away(0, i - window).wait_send()

        away(0, i).start()

    for k in range(chunks):
        own_in(k).start()

    one_real = branch_one[0].astype(jnp.float32).T.astype(jnp.bfloat16)
    one_imag = branch_one[1].astype(jnp.float32).T.astype(jnp.bfloat16)
    w_one[:size_a, :size_a] = one_real
    w_one[:size_a, size_a:] = -one_imag
    w_one[size_a:, :size_a] = one_imag
    w_one[size_a:, size_a:] = one_real

    hot = lax.broadcasted_iota(jnp.int32, (size_r, size_r), 0) == mode_order[...]
    places = jnp.where(hot, 1.0, 0.0).astype(jnp.bfloat16)
    two_real = jnp.dot(places, branch_two[0], preferred_element_type=jnp.float32)
    two_imag = jnp.dot(places, branch_two[1], preferred_element_type=jnp.float32)
    w_two[:size_r, :size_r] = two_real.astype(jnp.bfloat16)
    w_two[:size_r, size_r:] = two_imag.astype(jnp.bfloat16)
    w_two[size_r:, :size_r] = (-two_imag).astype(jnp.bfloat16)
    w_two[size_r:, size_r:] = two_real.astype(jnp.bfloat16)

    pick = (closing.shape[2], close_ref.shape[1])
    picked = lax.broadcasted_iota(jnp.int32, pick, 0) == (
        lax.broadcasted_iota(jnp.int32, pick, 1) + me * lb
    )
    picked = jnp.where(picked, 1.0, 0.0).astype(jnp.bfloat16)
    for p in range(2):
        close_ref[p * size_a : (p + 1) * size_a] = jnp.dot(
            closing[p], picked, preferred_element_type=jnp.float32
        ).astype(jnp.bfloat16)

    width = 2 * n * cb
    for k in range(chunks):
        for part in range(2):
            pieces = []
            for s in range(n):
                piece = branch_three[:, s * lb + k * cb : s * lb + (k + 1) * cb, :].astype(
                    jnp.float32
                )
                pieces += [piece[0], -piece[1]] if part == 0 else [piece[1], piece[0]]
            stacked[part, :, k * width : (k + 1) * width] = (
                jnp.concatenate(pieces, axis=0).T.astype(jnp.bfloat16)
            )
    run = spread.shape[0] // 2
    for t in range(stacked.shape[1] // run):
        block = jnp.concatenate(
            [stacked[0, t * run : (t + 1) * run], stacked[1, t * run : (t + 1) * run]], axis=0
        )
        shuffled[2 * t * run : 2 * (t + 1) * run] = jnp.dot(
            spread[...], block, preferred_element_type=jnp.float32
        ).astype(jnp.bfloat16)
    weights_out().start()

    for k in range(chunks):
        own_in(k).wait()
        if k + 1 < chunks:
            @pl.loop(1, window + 1)
            def _(i):
                away(k, n - 1 - window + i).wait_send()
                stage(k + 1, i).wait()
                away(k + 1, i).start()

        def turn(s):
            for p in range(2):
                block = held[k, p, rows(s)].reshape(la * cb, size_r)
                moved = jnp.dot(to_b[...], block, preferred_element_type=jnp.float32)
                turned[:, pl.ds(pl.multiple_of(p * size_a + s * la, la), la), :] = (
                    moved.astype(jnp.bfloat16).reshape(cb, la, size_r)
                )

        turn(me)

        @pl.loop(1, n)
        def _(i):
            s = peer(i)
            arrival(k, s).wait_recv()
            turn(s)

        @pl.loop(0, cb)
        def _(b):
            mixed = jnp.dot(w_one[...], turned[b], preferred_element_type=jnp.float32)
            hot = lax.broadcasted_iota(jnp.int32, (close_ref.shape[1], size_r), 0) == k * cb + b
            gate = jnp.dot(
                close_ref[...],
                jnp.where(hot, 1.0, 0.0).astype(jnp.bfloat16),
                preferred_element_type=jnp.float32,
            )
            real_part, imag_part = mixed[:size_a], mixed[size_a:]
            gate_real, gate_imag = gate[:size_a], gate[size_a:]
            phased = jnp.concatenate(
                [
                    (gate_real * real_part - gate_imag * imag_part).astype(jnp.bfloat16),
                    (gate_real * imag_part + gate_imag * real_part).astype(jnp.bfloat16),
                ],
                axis=1,
            )
            both = jnp.dot(phased, w_two[...], preferred_element_type=jnp.float32).astype(
                jnp.bfloat16
            )
            turned[b, :size_a] = both[:, :size_r]
            turned[b, size_a:] = both[:, size_r:]
            if k + 1 < chunks:
                @pl.when(b < n - 1 - window)
                def _():
                    away(k + 1, b + 1).wait_send()
                    stage(k + 1, b + 1 + window).wait()
                    away(k + 1, b + 1 + window).start()

        def unturn(d):
            for p in range(2):
                block = turned[
                    :, pl.ds(pl.multiple_of(p * size_a + d * la, la), la), :
                ].reshape(cb * la, size_r)
                moved = jnp.dot(to_a[...], block, preferred_element_type=jnp.float32)
                held[k, p, rows(d)] = moved.astype(jnp.bfloat16).reshape(la, cb, size_r)

        @pl.loop(1, n)
        def _(i):
            unturn(peer(i))
            if k + 1 < chunks:
                @pl.when(i >= n - window)
                def _():
                    away(k + 1, i).wait_send()
            back(k, i).start()

        unturn(me)
        own_back(k).start()

    weights_out().wait()
    for k in range(chunks):
        own_back(k).wait()

        @pl.loop(1, n)
        def _(i):
            back(k, i).wait_send()
            back_arrival(k, peer(i)).wait_recv()


def close_kernel(block_ref, w_three, out_ref):
    chunks, n, two, steps, cb, size_q = block_ref.shape
    half = size_q // 2
    groups = out_ref.shape[0] // steps
    for a in range(steps):
        block = block_ref[:, :, :, a].reshape(chunks * n * two * cb, size_q)
        mixed = jnp.dot(w_three[...], block, preferred_element_type=jnp.float32)
        left = mixed[:, :half].reshape(groups, 8, half)
        right = mixed[:, half:].reshape(groups, 8, half)
        even = lax.broadcasted_iota(jnp.int32, left.shape, 1) % 2 == 0
        own = pl.ds(a * groups, groups)
        out_ref[own, 0] = jnp.where(even, left, pltpu.roll(right, 1, 1))
        out_ref[own, 1] = jnp.where(even, pltpu.roll(left, 7, 1), right)


def kernel_device(stem_tensor, branch_one, branch_two, mode_order, branch_three, closing):
    n = lax.axis_size("inter")
    _, la, size_b, _, size_r = stem_tensor.shape
    size_a = branch_one.shape[1]
    size_c = branch_three.shape[2]
    lb = size_b // n
    cb = lb // CHUNKS
    stem = stem_tensor.reshape(2, la, size_b, size_r)

    line = np.arange(la * cb)
    to_b = (
        ((line // la)[:, None] == (line % cb)[None, :])
        & ((line % la)[:, None] == (line // cb)[None, :])
    ).astype(np.float32)
    g, low, part, high = np.unravel_index(np.arange(2 * RUN), (RUN // 4, 2, 2, 2))
    spread = np.zeros((2 * RUN, 2 * RUN), np.float32)
    spread[np.arange(2 * RUN), part * RUN + 4 * g + 2 * high + low] = 1.0
    to_b, to_a, spread = (jnp.asarray(x, jnp.bfloat16) for x in (to_b, to_b.T, spread))

    vmem = pl.BlockSpec(memory_space=pltpu.VMEM)
    anywhere = pl.BlockSpec(memory_space=pl.ANY)
    returned, w_three = pl.pallas_call(
        functools.partial(swap_kernel, n),
        out_shape=[
            jax.ShapeDtypeStruct((CHUNKS, n, 2, la, cb, size_r), jnp.bfloat16),
            jax.ShapeDtypeStruct((2 * size_c, 2 * size_b), jnp.bfloat16),
        ],
        in_specs=[anywhere] + [vmem] * 8,
        out_specs=[anywhere, anywhere],
        scratch_shapes=[
            pltpu.VMEM((CHUNKS, n, 2, la, cb, size_r), jnp.bfloat16),
            pltpu.VMEM((CHUNKS, 2, size_a, cb, size_r), jnp.bfloat16),
            pltpu.VMEM((cb, 2 * size_a, size_r), jnp.bfloat16),
            pltpu.VMEM((2 * size_a, 2 * size_a), jnp.bfloat16),
            pltpu.VMEM((2 * size_r, 2 * size_r), jnp.bfloat16),
            pltpu.VMEM((2 * size_a, pl.cdiv(lb, 128) * 128), jnp.bfloat16),
            pltpu.VMEM((2, size_c, 2 * size_b), jnp.bfloat16),
            pltpu.VMEM((2 * size_c, 2 * size_b), jnp.bfloat16),
            pltpu.SemaphoreType.DMA((CHUNKS, n)),
            pltpu.SemaphoreType.DMA((CHUNKS, n)),
            pltpu.SemaphoreType.DMA((CHUNKS, n)),
            pltpu.SemaphoreType.DMA((CHUNKS, n)),
            pltpu.SemaphoreType.DMA((CHUNKS, n)),
            pltpu.SemaphoreType.DMA((3, CHUNKS)),
        ],
        compiler_params=pltpu.CompilerParams(
            collective_id=0, has_side_effects=True, vmem_limit_bytes=62 * 1024 * 1024
        ),
        cost_estimate=pl.CostEstimate(
            flops=24 * size_a * size_a * lb * size_r,
            bytes_accessed=16 * size_a * lb * size_r,
            transcendentals=0,
        ),
    )(
        stem, branch_one, branch_two, mode_order.reshape(1, size_r), branch_three, closing,
        to_b, to_a, spread,
    )

    groups = size_c // 4
    half = size_r // 2
    steps = 4
    out = pl.pallas_call(
        close_kernel,
        grid=(la // steps,),
        out_shape=jax.ShapeDtypeStruct((la * groups, 2, 8, half), jnp.float32),
        in_specs=[
            pl.BlockSpec((CHUNKS, n, 2, steps, cb, size_r), lambda a: (0, 0, 0, a, 0, 0)),
            pl.BlockSpec((2 * size_c, 2 * size_b), lambda a: (0, 0)),
        ],
        out_specs=pl.BlockSpec((steps * groups, 2, 8, half), lambda a: (a, 0, 0, 0)),
        compiler_params=pltpu.CompilerParams(vmem_limit_bytes=56 * 1024 * 1024),
        cost_estimate=pl.CostEstimate(
            flops=8 * la * size_b * size_c * size_r,
            bytes_accessed=la * (4 * size_b + 8 * size_c) * size_r,
            transcendentals=0,
        ),
    )(returned, w_three)
    return out.reshape(la, size_c, 2, 1, size_r)


def on_device(stem_tensor, branch_one, branch_two, mode_order, branch_three, closing):
    n = lax.axis_size("inter")
    _, la, size_b, amps, size_r = stem_tensor.shape
    lb = size_b // n
    fits = (
        amps == 1
        and n % 2 == 0
        and n - 1 - min(WINDOW, n - 1) <= lb // CHUNKS
        and la % 16 == 0
        and lb % (16 * CHUNKS) == 0
        and size_r == 256
        and branch_one.shape[1] % 16 == 0
        and branch_three.shape[2] % RUN == 0
    )
    device = kernel_device if fits else plain_device
    return device(stem_tensor, branch_one, branch_two, mode_order, branch_three, closing)


def solution(mesh):
    in_specs = (P(None, ("cuts", "inter"), None, None, None), P(), P(), P(), P(), P())
    out_specs = P(("cuts", "inter"), None, None, None, None)
    return jax.shard_map(
        on_device, mesh=mesh, in_specs=in_specs, out_specs=out_specs, check_vma=False
    )
```
